256 devices in a mesh: group: 8 (over y, x_hi), row: 32 (over x_lo, z, core).
Axes of the slice: x: 4 (x_hi: 2, x_lo: 2; x = x_hi * 2 + x_lo), y: 4, z: 8, core: 2. Of those that a mesh axis runs over, the one named last changes fastest.
Arguments:
- embeddings: bfloat16 [1048576, 128], P(('group', 'row')), parts along dimension 0, may hold values from -6 to 6
- band_tiles: bfloat16 [8192, 4, 128, 128], P(('group', 'row')), parts along dimension 0, may hold values from -0.1875 to 0.1875
- band_offsets: int32 [8192, 4], P(('group', 'row')), parts along dimension 0, may hold values from -3 to 3
- hub_tiles: bfloat16 [8192, 4, 128, 128], P(('group', 'row')), parts along dimension 0, may hold values from -0.1875 to 0.1875
- hub_blocks: int32 [8192, 4], P(('group', 'row')), parts along dimension 0, may hold values from 0 to 31, all different within a row
- hub_ids: int32 [3, 32768], P(None, ('group', 'row')), parts along dimension 1, may hold values from 0 to 131071, as said below
Outputs:
- averaged: bfloat16 [1048576, 128], P(('group', 'row')), parts along dimension 0
The draws below stay inside these ranges and needn't reach their ends.
There are 8 independent parts, one for each index of `group`. The reference program is written for one: setup_inputs(seed, part) draws one part's arguments, and reference() takes and returns one part's arrays. A program takes and returns all parts, laid end to end along the dimension named above; each array names one. Nothing has to cross between parts.
Inputs may be any that keep to these rules, and one draw needn't show every extreme that they name: `hub_ids`: in each layer, entries k * 128 to (k+1) * 128 - 1 are distinct rows among k * 4096 to (k+1) * 4096 - 1.
All inputs are finite; a program needn't handle non-finite values.
Results may differ from the reference program's by a relative error of at most 0.0075.
Values may be sent and summed in bfloat16 or wider, within the bound.
No kernel may reach another device: no remote copies, remote signals or barrier semaphores. Data moves between devices by JAX's collectives and lax.ppermute only.
A program may use at most 64 MiB of HBM per device.

```python
import jax
import jax.numpy as jnp
from jax import lax

FEAT = 128
BLK = 128
BAND = 3
K_BAND = 4
K_HUB = 4
LAYERS = 3
HUB_DEV = 128
ROWS_DEV = 4096
ROWS = 131072
HUB = 4096


def draw_hub_ids(key, part):
    device_count = HUB // HUB_DEV
    total_lists = LAYERS * device_count

    def one_list(list_number):
        sub_key = jax.random.fold_in(key, list_number)
        device = list_number % device_count
        order = jax.random.permutation(sub_key, ROWS_DEV).astype(jnp.int32)
        target = jnp.where(device == 0, 0, jnp.where(device == device_count - 1, ROWS_DEV - 1, -1))
        position = jnp.argmax(order == target).astype(jnp.int32)
        leading = order[0]
        order = order.at[position].set(leading)
        order = order.at[0].set(jnp.where(target >= 0, target, leading))
        return order[:HUB_DEV] + device * ROWS_DEV
    lists = jax.vmap(one_list)(jnp.arange(total_lists, dtype=jnp.int32))
    return lists.reshape(LAYERS, HUB).astype(jnp.int32)


def set_ends(drawn, own_key, least, largest):
    spot = [jax.random.randint(jax.random.fold_in(own_key, axis), (), 0, length) for axis, length in enumerate(drawn.shape)]
    widest = drawn.shape.index(max(drawn.shape))
    beside = spot[:widest] + [(spot[widest] + 1) % drawn.shape[widest]] + spot[widest + 1:]
    return drawn.at[tuple(spot)].set(least).at[tuple(beside)].set(largest)


def steps_of(rng, shape, pieces, low, high):
    gain, own = 1.0, jax.random.fold_in(rng, 6)
    for axis_at, blocks in pieces:
        heights = jnp.exp(jax.random.uniform(jax.random.fold_in(own, axis_at), (blocks,), jnp.float32, low / len(pieces), high / len(pieces)))
        gain = gain * jnp.repeat(heights, shape[axis_at] // blocks).reshape([-1 if axis == axis_at else 1 for axis in range(len(shape))])
    return gain


def picks_of(key, rows, amount, top, lift):
    sequence = jax.random.permutation(jax.random.fold_in(key, 1), amount)
    favour = sequence
    for power in range(3):
        favour = favour * favour // amount
    favour = favour * lift // amount
    chance = jax.random.randint(jax.random.fold_in(key, 2), (rows, amount), 0, 4096) + favour
    fixed_rows = jax.random.permutation(jax.random.fold_in(key, 3), rows)[jnp.arange(amount) % rows]
    chance = jnp.where(jnp.arange(rows)[:, None] == fixed_rows[None, :], 1 << 14, chance)
    priority = chance * amount + jnp.arange(amount)
    return lax.top_k(priority.astype(jnp.int32), top)[1].astype(jnp.int32)


def scatter_about(rng, shape, deviation, most, split=(), kind=jnp.bfloat16):
    entries = jax.random.normal(rng, shape, jnp.float32) * deviation
    if len(split) > 0:
        entries = steps_of(rng, shape, split, -0.22, 0.18) * entries
    return jnp.clip(entries, min=-most, max=most).astype(kind)


def setup_inputs(seed: int = 0, part: int = 0) -> dict:
    key_list = jax.random.split(jax.random.key(seed), 7)
    part_splits = jax.random.split(jax.random.fold_in(key_list[6], part), 7)
    return {
        "embeddings": scatter_about(part_splits[0], (ROWS, FEAT), 1.0, 6.0, ((0, 32),)),
        "band_tiles": scatter_about(part_splits[1], (ROWS // BLK, K_BAND, BLK, BLK), ((K_BAND + K_HUB) * BLK) ** -0.5, 0.1875, ((0, 32),)),
        "band_offsets": set_ends(jax.random.randint(part_splits[2], (ROWS // BLK, K_BAND), 0 - BAND, BAND + 1), jax.random.fold_in(part_splits[2], 1), 0 - BAND, BAND).astype(jnp.int32),
        "hub_tiles": scatter_about(part_splits[3], (ROWS // BLK, K_HUB, BLK, BLK), ((K_BAND + K_HUB) * BLK) ** -0.5, 0.1875, ((0, 32),)),
        "hub_blocks": picks_of(part_splits[4], (ROWS // BLK), HUB // BLK, K_HUB, 0),
        "hub_ids": draw_hub_ids(jax.random.fold_in(jax.random.fold_in(key_list[6], part), 71), part),
    }


def propagate(current, band_tiles, band_offsets, hub_tiles, hub_blocks, level_ids):
    block_count = ROWS // BLK
    blocks = current.reshape(block_count, BLK, FEAT)
    zero_rim = jnp.zeros((BAND, BLK, FEAT), current.dtype)
    padded = jnp.concatenate([zero_rim, blocks, zero_rim], axis=0)
    block_index = (jnp.arange(block_count, dtype=jnp.int32)[:, None] + band_offsets + BAND).astype(jnp.int32)
    nearby = padded[block_index]
    band_part = jnp.einsum("bkij,bkjf->bif", band_tiles.astype(jnp.float32), nearby.astype(jnp.float32))
    hub_panel = current[level_ids].reshape(HUB // BLK, BLK, FEAT)
    hub_near = hub_panel[hub_blocks]
    hub_part = jnp.einsum("bkij,bkjf->bif", hub_tiles.astype(jnp.float32), hub_near.astype(jnp.float32))
    return (band_part + hub_part).reshape(ROWS, FEAT).astype(jnp.bfloat16)


def reference(embeddings, band_tiles, band_offsets, hub_tiles, hub_blocks, hub_ids):
    current = embeddings
    layer_sum = embeddings.astype(jnp.float32)
    for level_index in range(LAYERS):
        current = propagate(current, band_tiles, band_offsets, hub_tiles, hub_blocks, hub_ids[level_index])
        layer_sum = layer_sum + current.astype(jnp.float32)
    return (layer_sum / (LAYERS + 1.0)).astype(jnp.bfloat16)
```

```python
import functools

import jax
import jax.numpy as jnp
from jax import lax
from jax.experimental import pallas as pl
from jax.experimental.pallas import tpu as pltpu
from jax.sharding import PartitionSpec as P

BAND = 3
LAYERS = 3
BLOCK = 128
STEP = 4
DEVICES = 32


def index_of(x, z, c):
    return x * 16 + z * 2 + c


def permutation(move):
    return [
        (index_of(x, z, c), index_of(*move(x, z, c)))
        for x in range(2)
        for z in range(8)
        for c in range(2)
    ]


def along_z(step):
    return permutation(lambda x, z, c: (x, z ^ step, c))


ACROSS_X = permutation(lambda x, z, c: (1 - x, z, c))
ACROSS_CORE = permutation(lambda x, z, c: (x, z, 1 - c))
ACROSS_EDGE = [
    (i, (i + 1) % DEVICES if i % 2 else (i - 1) % DEVICES) for i in range(DEVICES)
]


def permute(array, pairs):
    return lax.ppermute(array, "row", pairs)


def gather_rows(own):
    pair = jnp.concatenate([own, permute(own, along_z(6))])
    column = jnp.concatenate([pair] + [permute(pair, along_z(g)) for g in (1, 2, 3)])
    plane = jnp.concatenate([column, permute(column, ACROSS_X)])
    return jnp.concatenate([plane, permute(plane, ACROSS_CORE)])


def places(hub_blocks, me):
    delta = hub_blocks ^ me
    dx, dz, dc = delta >> 4, (delta >> 1) & 7, delta & 1
    s = dz >> 2
    g = (dz & 3) ^ (2 * s)
    return 16 * dc + 8 * dx + 2 * g + s


def dot(a, b):
    return jnp.dot(a, b, preferred_element_type=jnp.float32)


def one_hot(ids, first, width):
    columns = lax.broadcasted_iota(jnp.int32, (ids.shape[0], width), 1) + first
    return (columns == ids).astype(jnp.bfloat16)


def pick_kernel(ids_ref, table_ref, out_ref):
    rows = table_ref.shape[0]
    wide = 2 * BLOCK
    ids = ids_ref[...]
    total = jnp.zeros(out_ref.shape, jnp.float32)
    for first in range(0, rows, wide):
        total += dot(one_hot(ids, first, wide), table_ref[first : first + wide, :])
    out_ref[...] = total.astype(out_ref.dtype)


def pick(ids, table):
    return pl.pallas_call(
        pick_kernel,
        out_shape=jax.ShapeDtypeStruct((ids.shape[0], table.shape[1]), table.dtype),
        cost_estimate=pl.CostEstimate(flops=2**27, bytes_accessed=2**20, transcendentals=0),
    )(ids, table)


def band_kernel(offsets_ref, side_ref, table_ref, inner_ref, outer_ref, tiles_ref, out_ref, padded):
    step = pl.program_id(0)
    blocks = table_ref.shape[0]

    @pl.when(step == 0)
    def _():
        padded[BAND : BAND + blocks] = table_ref[...]
        core, has_left, has_right = side_ref[0], side_ref[1], side_ref[2]
        inner, outer = inner_ref[...], outer_ref[...]
        left = jnp.where(core == 0, outer, inner)
        right = jnp.where(core == 0, inner, outer)
        padded[0:BAND] = jnp.where(has_left == 1, left, jnp.zeros_like(left))
        padded[BAND + blocks :] = jnp.where(has_right == 1, right, jnp.zeros_like(right))

    for i in range(STEP):
        b = step * STEP + i
        tiles = jnp.concatenate([tiles_ref[i, k] for k in range(4)], axis=1)
        near = jnp.concatenate(
            [padded[b + BAND + offsets_ref[b * 4 + k]] for k in range(4)], axis=0
        )
        out_ref[i] = dot(tiles, near)


def band_products(offsets, side, table, inner, outer, tiles):
    blocks = table.shape[0]
    whole = lambda shape: pl.BlockSpec(shape, lambda i, *_: (0,) * len(shape))
    return pl.pallas_call(
        band_kernel,
        grid_spec=pltpu.PrefetchScalarGridSpec(
            num_scalar_prefetch=2,
            grid=(blocks // STEP,),
            in_specs=[
                whole(table.shape),
                whole(inner.shape),
                whole(outer.shape),
                pl.BlockSpec((STEP, 4, BLOCK, BLOCK), lambda i, *_: (i, 0, 0, 0)),
            ],
            out_specs=pl.BlockSpec((STEP, BLOCK, BLOCK), lambda i, *_: (i, 0, 0)),
            scratch_shapes=[pltpu.VMEM((blocks + 2 * BAND, BLOCK, BLOCK), jnp.bfloat16)],
        ),
        out_shape=jax.ShapeDtypeStruct((blocks, BLOCK, BLOCK), jnp.float32),
        compiler_params=pltpu.CompilerParams(vmem_limit_bytes=24 * 2**20),
        cost_estimate=pl.CostEstimate(flops=2**29, bytes_accessed=7 * 2**20, transcendentals=0),
    )(offsets, side, table, inner, outer, tiles)


def hub_sum(i, step, place_ref, panel_ref, tiles_ref, band_ref):
    b = step * STEP + i
    tiles = jnp.concatenate([tiles_ref[i, k] for k in range(4)], axis=1)
    near = jnp.concatenate([panel_ref[place_ref[b * 4 + k]] for k in range(4)], axis=0)
    return (dot(tiles, near) + band_ref[i]).astype(jnp.bfloat16)


def hub_kernel(place_ref, ids_ref, panel_ref, tiles_ref, band_ref, out_ref, picked_ref, total):
    step = pl.program_id(0)

    @pl.when(step == 0)
    def _():
        total[...] = jnp.zeros_like(total)

    ids = ids_ref[...]
    for i in range(STEP):
        value = hub_sum(i, step, place_ref, panel_ref, tiles_ref, band_ref)
        out_ref[i] = value
        total[...] += dot(one_hot(ids, (step * STEP + i) * BLOCK, BLOCK), value)

    @pl.when(step == pl.num_programs(0) - 1)
    def _():
        picked_ref[...] = total[...].astype(jnp.bfloat16)


def last_kernel(place_ref, panel_ref, tiles_ref, band_ref, e0_ref, e1_ref, e2_ref, out_ref):
    step = pl.program_id(0)
    for i in range(STEP):
        value = hub_sum(i, step, place_ref, panel_ref, tiles_ref, band_ref)
        total = e0_ref[i].astype(jnp.float32) + e1_ref[i].astype(jnp.float32)
        total = total + e2_ref[i].astype(jnp.float32) + value.astype(jnp.float32)
        out_ref[i] = (total * 0.25).astype(jnp.bfloat16)


def rows_spec():
    return pl.BlockSpec((STEP, BLOCK, BLOCK), lambda i, *_: (i, 0, 0))


def tiles_spec():
    return pl.BlockSpec((STEP, 4, BLOCK, BLOCK), lambda i, *_: (i, 0, 0, 0))


def hub_layer(place, ids, panel, tiles, band):
    blocks = tiles.shape[0]
    return pl.pallas_call(
        hub_kernel,
        grid_spec=pltpu.PrefetchScalarGridSpec(
            num_scalar_prefetch=1,
            grid=(blocks // STEP,),
            in_specs=[
                pl.BlockSpec(ids.shape, lambda i, *_: (0, 0)),
                pl.BlockSpec(panel.shape, lambda i, *_: (0, 0, 0)),
                tiles_spec(),
                rows_spec(),
            ],
            out_specs=[rows_spec(), pl.BlockSpec((BLOCK, BLOCK), lambda i, *_: (0, 0))],
            scratch_shapes=[pltpu.VMEM((BLOCK, BLOCK), jnp.float32)],
        ),
        out_shape=[
            jax.ShapeDtypeStruct((blocks, BLOCK, BLOCK), jnp.bfloat16),
            jax.ShapeDtypeStruct((BLOCK, BLOCK), jnp.bfloat16),
        ],
        compiler_params=pltpu.CompilerParams(vmem_limit_bytes=24 * 2**20),
        cost_estimate=pl.CostEstimate(flops=2**29, bytes_accessed=8 * 2**20, transcendentals=0),
    )(place, ids, panel, tiles, band)


def last_layer(place, panel, tiles, band, e0, e1, e2):
    blocks = tiles.shape[0]
    return pl.pallas_call(
        last_kernel,
        grid_spec=pltpu.PrefetchScalarGridSpec(
            num_scalar_prefetch=1,
            grid=(blocks // STEP,),
            in_specs=[
                pl.BlockSpec(panel.shape, lambda i, *_: (0, 0, 0)),
                tiles_spec(),
            ]
            + [rows_spec()] * 4,
            out_specs=rows_spec(),
        ),
        out_shape=jax.ShapeDtypeStruct((blocks, BLOCK, BLOCK), jnp.bfloat16),
        compiler_params=pltpu.CompilerParams(vmem_limit_bytes=24 * 2**20),
        cost_estimate=pl.CostEstimate(flops=2**29, bytes_accessed=11 * 2**20, transcendentals=0),
    )(place, panel, tiles, band, e0, e1, e2)


def body(embeddings, band_tiles, band_offsets, hub_tiles, hub_blocks, hub_ids):
    rows_dev, features = embeddings.shape
    blocks = rows_dev // BLOCK
    me = lax.axis_index("row")
    core = me % 2
    side = jnp.stack([core, (me > 0).astype(jnp.int32), (me < DEVICES - 1).astype(jnp.int32)])
    offsets = band_offsets.reshape(-1)
    place = places(hub_blocks, me).reshape(-1)
    ids = (hub_ids - me * rows_dev)[:, :, None]

    def halos(table):
        start_inner = jnp.where(core == 0, blocks - BAND, 0)
        start_outer = jnp.where(core == 0, 0, blocks - BAND)
        inner = permute(lax.dynamic_slice_in_dim(table, start_inner, BAND), ACROSS_CORE)
        outer = permute(lax.dynamic_slice_in_dim(table, start_outer, BAND), ACROSS_EDGE)
        return inner, outer

    tables = [embeddings.reshape(blocks, BLOCK, features)]
    picked = pick(ids[0], embeddings)
    for level in range(LAYERS):
        table = tables[-1]
        panel = gather_rows(picked).reshape(DEVICES, BLOCK, features)
        inner, outer = halos(table)
        band = band_products(offsets, side, table, inner, outer, band_tiles)
        if level < LAYERS - 1:
            table, picked = hub_layer(place, ids[level + 1], panel, hub_tiles, band)
            tables.append(table)
        else:
            averaged = last_layer(place, panel, hub_tiles, band, *tables)
    return averaged.reshape(rows_dev, features)


def solution(mesh):
    return jax.shard_map(
        body,
        mesh=mesh,
        in_specs=(
            P(("group", "row"), None),
            P(("group", "row"), None, None, None),
            P(("group", "row"), None),
            P(("group", "row"), None, None, None),
            P(("group", "row"), None),
            P(None, ("group", "row")),
        ),
        out_specs=P(("group", "row"), None),
        check_vma=False,
    )
```

```python
import functools

import jax
import jax.numpy as jnp
from jax import lax
from jax.experimental import pallas as pl
from jax.experimental.pallas import tpu as pltpu
from jax.sharding import PartitionSpec as P

BAND = 3
LAYERS = 3
BLOCK = 128
STEP = 4
DEVICES = 32


def index_of(x, z, c):
    return x * 16 + z * 2 + c


def permutation(move):
    return [
        (index_of(x, z, c), index_of(*move(x, z, c)))
        for x in range(2)
        for z in range(8)
        for c in range(2)
    ]


def along_z(step):
    return permutation(lambda x, z, c: (x, z ^ step, c))


ACROSS_X = permutation(lambda x, z, c: (1 - x, z, c))
ACROSS_CORE = permutation(lambda x, z, c: (x, z, 1 - c))
ACROSS_EDGE = [
    (i, (i + 1) % DEVICES if i % 2 else (i - 1) % DEVICES) for i in range(DEVICES)
]


def permute(array, pairs):
    return lax.ppermute(array, "row", pairs)


def places(hub_blocks, me):
    delta = hub_blocks ^ me
    dx, dz, dc = delta >> 4, (delta >> 1) & 7, delta & 1
    s = dz >> 2
    g = (dz & 3) ^ (2 * s)
    return 16 * dc + 8 * dx + 2 * g + s


def dot(a, b):
    return jnp.dot(a, b, preferred_element_type=jnp.float32)


def id_columns(ids_ref, level, first):
    row = ids_ref[level : level + 1, :] - first
    return jnp.transpose(jnp.broadcast_to(row, (BLOCK, BLOCK)))


def one_hot(ids, first, count):
    column = lax.broadcasted_iota(jnp.int32, (BLOCK, BLOCK), 1) + first
    parts = [(column + i * BLOCK == ids).astype(jnp.bfloat16) for i in range(count)]
    return jnp.concatenate(parts, axis=1)


def call(kernel, out_shape, scalars, arrays, flops, scratch=()):
    smem = pl.BlockSpec(memory_space=pltpu.SMEM)
    vmem = pl.BlockSpec(memory_space=pltpu.VMEM)
    moved = sum(a.size * a.dtype.itemsize for a in arrays)
    return pl.pallas_call(
        kernel,
        in_specs=[smem] * len(scalars) + [vmem] * len(arrays),
        out_specs=jax.tree.map(lambda _: vmem, out_shape),
        out_shape=out_shape,
        scratch_shapes=list(scratch),
        compiler_params=pltpu.CompilerParams(vmem_limit_bytes=40 * 2**20),
        cost_estimate=pl.CostEstimate(flops=flops, bytes_accessed=moved, transcendentals=0),
    )(*scalars, *arrays)


def f32(*shape):
    return jax.ShapeDtypeStruct(shape, jnp.float32)


def bf16(*shape):
    return jax.ShapeDtypeStruct(shape, jnp.bfloat16)


def pick_kernel(side_ref, ids_ref, table_ref, out_ref):
    ids = id_columns(ids_ref, 0, side_ref[3])
    total = jnp.zeros(out_ref.shape, jnp.float32)
    for b in range(0, table_ref.shape[0], STEP):
        table = table_ref[b : b + STEP].reshape(STEP * BLOCK, -1)
        total += dot(one_hot(ids, b * BLOCK, STEP), table)
    out_ref[...] = total.astype(out_ref.dtype)


def expand_kernel(side_ref, place_ref, ids_ref, tiles_ref, *out_refs):
    columns = [id_columns(ids_ref, level + 1, side_ref[3]) for level in range(len(out_refs))]
    for out_ref in out_refs:
        out_ref[...] = jnp.zeros_like(out_ref)

    def group(step, carry):
        for i in range(STEP):
            b = step * STEP + i
            rows = jnp.concatenate([one_hot(c, b * BLOCK, 1) for c in columns], axis=0)
            tiles = jnp.concatenate([tiles_ref[b, k] for k in range(4)], axis=1)
            taken = dot(rows, tiles).astype(jnp.bfloat16)
            for k in range(4):
                place = place_ref[b * 4 + k]
                for n, out_ref in enumerate(out_refs):
                    part = taken[n * BLOCK : (n + 1) * BLOCK, k * BLOCK : (k + 1) * BLOCK]
                    out_ref[place] += part
        return carry

    lax.fori_loop(0, tiles_ref.shape[0] // STEP, group, 0)


def tile_sum(b, tiles_ref, blocks):
    tiles = jnp.concatenate([tiles_ref[b, k] for k in range(4)], axis=1)
    return dot(tiles, jnp.concatenate(blocks, axis=0))


def band_kernel(level, offsets_ref, side_ref, table_ref, inner_ref, outer_ref, tiles_ref, ids_ref, *rest):
    out_ref, padded = rest[0], rest[-1]
    blocks = table_ref.shape[0]
    padded[BAND : BAND + blocks] = table_ref[...]
    core, has_left, has_right = side_ref[0], side_ref[1], side_ref[2]
    inner, outer = inner_ref[...], outer_ref[...]
    left = jnp.where(core == 0, outer, inner)
    right = jnp.where(core == 0, inner, outer)
    padded[0:BAND] = jnp.where(has_left == 1, left, jnp.zeros_like(left))
    padded[BAND + blocks :] = jnp.where(has_right == 1, right, jnp.zeros_like(right))
    if level is not None:
        ids = id_columns(ids_ref, level, side_ref[3])
        rest[1][...] = jnp.zeros_like(rest[1])

    def group(step, carry):
        values = []
        for i in range(STEP):
            b = step * STEP + i
            near = [padded[b + BAND + offsets_ref[b * 4 + k]] for k in range(4)]
            values.append(tile_sum(b, tiles_ref, near))
            out_ref[b] = values[-1]
        if level is not None:
            value = jnp.concatenate(values, axis=0)
            high = value.astype(jnp.bfloat16)
            low = (value - high.astype(jnp.float32)).astype(jnp.bfloat16)
            hot = one_hot(ids, step * STEP * BLOCK, STEP)
            both = dot(hot, jnp.concatenate([high, low], axis=1))
            rest[1][...] += both[:, :BLOCK] + both[:, BLOCK:]
        return carry

    lax.fori_loop(0, blocks // STEP, group, 0)


def band_products(level, offsets, side, table, inner, outer, tiles, ids):
    blocks = table.shape[0]
    return call(
        functools.partial(band_kernel, level),
        [f32(blocks, BLOCK, BLOCK)] + ([] if level is None else [f32(BLOCK, BLOCK)]),
        (offsets, side),
        (table, inner, outer, tiles, ids),
        2**29,
        [pltpu.VMEM((blocks + 2 * BAND, BLOCK, BLOCK), jnp.bfloat16)],
    )


def hub_kernel(place_ref, p0_ref, p1_ref, p2_ref, p3_ref, tiles_ref, band_ref, *rest):
    out_ref, panel = rest[-2], rest[-1]
    earlier = rest[:-2]
    for n, ref in enumerate((p0_ref, p1_ref, p2_ref, p3_ref)):
        panel[8 * n : 8 * n + 8] = ref[...].reshape(8, BLOCK, BLOCK)

    def group(step, carry):
        for i in range(STEP):
            b = step * STEP + i
            near = [panel[place_ref[b * 4 + k]] for k in range(4)]
            value = (tile_sum(b, tiles_ref, near) + band_ref[b]).astype(jnp.bfloat16)
            if earlier:
                total = value.astype(jnp.float32)
                for ref in earlier:
                    total = total + ref[b].astype(jnp.float32)
                value = (total * 0.25).astype(jnp.bfloat16)
            out_ref[b] = value
        return carry

    lax.fori_loop(0, tiles_ref.shape[0] // STEP, group, 0)


def hub_layer(place, pieces, tiles, band, earlier=()):
    blocks = tiles.shape[0]
    return call(
        hub_kernel,
        bf16(blocks, BLOCK, BLOCK),
        (place,),
        (*pieces, tiles, band, *earlier),
        2**29,
        [pltpu.VMEM((DEVICES, BLOCK, BLOCK), jnp.bfloat16)],
    )


def row_sum(spread_ref, first, piece_ref):
    spread = jnp.concatenate([spread_ref[first + i] for i in range(8)], axis=1)
    return dot(spread, piece_ref[...])


def part_kernel(near_ref, spread_ref, p0_ref, p1_ref, p2_ref, out_ref):
    total = near_ref[...]
    for n, ref in enumerate((p0_ref, p1_ref, p2_ref)):
        total += row_sum(spread_ref, 8 * n, ref)
    out_ref[...] = total


def close_kernel(part_ref, spread_ref, p3_ref, out_ref):
    out_ref[...] = (part_ref[...] + row_sum(spread_ref, 24, p3_ref)).astype(jnp.bfloat16)


def together(*arrays):
    return lax.optimization_barrier(arrays)


def body(embeddings, band_tiles, band_offsets, hub_tiles, hub_blocks, hub_ids):
    rows_dev, features = embeddings.shape
    blocks = rows_dev // BLOCK
    me = lax.axis_index("row")
    core = me % 2
    side = jnp.stack([core, (me > 0).astype(jnp.int32), (me < DEVICES - 1).astype(jnp.int32), me * rows_dev])
    offsets = band_offsets.reshape(-1)
    place = places(hub_blocks, me).reshape(-1)

    def edges(table):
        inner = lax.dynamic_slice_in_dim(table, jnp.where(core == 0, blocks - BAND, 0), BAND)
        outer = lax.dynamic_slice_in_dim(table, jnp.where(core == 0, 0, blocks - BAND), BAND)
        return inner, outer

    tables = [embeddings.reshape(blocks, BLOCK, features)]
    picked = call(pick_kernel, bf16(BLOCK, features), (side,), (hub_ids, tables[0]), 2**27)
    pieces = band = None
    for level in range(LAYERS):
        last = level == LAYERS - 1
        if level == 0:
            picked, tiles, table = together(picked, hub_tiles, tables[0])
            across = permute(picked, along_z(6))
            spreads = call(
                expand_kernel,
                [bf16(DEVICES, BLOCK, BLOCK)] * (LAYERS - 1),
                (side, place),
                (hub_ids, tiles),
                2**30,
            )
            across, *spreads = together(across, *spreads)
        else:
            picked, band, *pieces = together(picked, band, *pieces)
            across = permute(picked, along_z(6))
            table = hub_layer(place, pieces, hub_tiles, band)
            across, table = together(across, table)
            tables.append(table)
        pair, table = together(jnp.concatenate([picked, across]), table)
        inner, outer = edges(table)
        inner = permute(inner, ACROSS_CORE)
        outer = permute(outer, ACROSS_EDGE)
        near = [permute(pair, along_z(g)) for g in (1, 2, 3)]
        inner, outer, *near = together(inner, outer, *near)
        column, inner, outer = together(jnp.concatenate([pair] + near), inner, outer)
        core_column = permute(column, ACROSS_CORE)
        x_column = permute(column, ACROSS_X)
        band, *rows = band_products(
            None if last else level + 1, offsets, side, table, inner, outer, band_tiles, hub_ids
        )
        core_column, x_column, band, *rows = together(core_column, x_column, band, *rows)
        far_column = permute(x_column, ACROSS_CORE)
        pieces = [column, x_column, core_column, far_column]
        if last:
            return hub_layer(place, pieces, hub_tiles, band, tables).reshape(rows_dev, features)
        spread = spreads[level]
        part = call(
            part_kernel, f32(BLOCK, features), (), (rows[0], spread, column, x_column, core_column), 2**27
        )
        picked = call(close_kernel, bf16(BLOCK, features), (), (part, spread, far_column), 2**25)


def solution(mesh):
    return jax.shard_map(
        body,
        mesh=mesh,
        in_specs=(
            P(("group", "row"), None),
            P(("group", "row"), None, None, None),
            P(("group", "row"), None),
            P(("group", "row"), None, None, None),
            P(("group", "row"), None),
            P(None, ("group", "row")),
        ),
        out_specs=P(("group", "row"), None),
        check_vma=False,
    )
```

```python
import functools

import jax
import jax.numpy as jnp
from jax import lax
from jax.experimental import pallas as pl
from jax.experimental.pallas import tpu as pltpu
from jax.sharding import PartitionSpec as P

BAND = 3
LAYERS = 3
BLOCK = 128
STEP = 16
CHUNK = 8
DEVICES = 32


def index_of(x, z, c):
    return x * 16 + z * 2 + c


def permutation(move):
    return [
        (index_of(x, z, c), index_of(*move(x, z, c)))
        for x in range(2)
        for z in range(8)
        for c in range(2)
    ]


def along_z(step):
    return permutation(lambda x, z, c: (x, z ^ step, c))


ACROSS_X = permutation(lambda x, z, c: (1 - x, z, c))
ACROSS_CORE = permutation(lambda x, z, c: (x, z, 1 - c))
ACROSS_EDGE = [
    (i, (i + 1) % DEVICES if i % 2 else (i - 1) % DEVICES) for i in range(DEVICES)
]


def permute(array, pairs):
    return lax.ppermute(array, "row", pairs)


def places(hub_blocks, me):
    delta = hub_blocks ^ me
    dx, dz, dc = delta >> 4, (delta >> 1) & 7, delta & 1
    s = dz >> 2
    g = (dz & 3) ^ (2 * s)
    return 16 * dc + 8 * dx + 2 * g + s


def dot(a, b):
    return jnp.dot(a, b, preferred_element_type=jnp.float32)


def id_columns(ids_ref, level, first):
    row = ids_ref[level : level + 1, :] - first
    return jnp.transpose(jnp.broadcast_to(row, (BLOCK, BLOCK)))


def one_hot(ids, first, count):
    column = lax.broadcasted_iota(jnp.int32, (BLOCK, BLOCK), 1) + first
    parts = [(column + i * BLOCK == ids).astype(jnp.bfloat16) for i in range(count)]
    return jnp.concatenate(parts, axis=1)


def call(kernel, out_shape, scalars, arrays, flops, scratch=()):
    smem = pl.BlockSpec(memory_space=pltpu.SMEM)
    vmem = pl.BlockSpec(memory_space=pltpu.VMEM)
    moved = sum(a.size * a.dtype.itemsize for a in arrays)
    return pl.pallas_call(
        kernel,
        in_specs=[smem] * len(scalars) + [vmem] * len(arrays),
        out_specs=jax.tree.map(lambda _: vmem, out_shape),
        out_shape=out_shape,
        scratch_shapes=list(scratch),
        compiler_params=pltpu.CompilerParams(vmem_limit_bytes=8 * 2**20),
        cost_estimate=pl.CostEstimate(flops=1, bytes_accessed=1, transcendentals=0),
    )(*scalars, *arrays)


def f32(*shape):
    return jax.ShapeDtypeStruct(shape, jnp.float32)


def bf16(*shape):
    return jax.ShapeDtypeStruct(shape, jnp.bfloat16)


def pick_kernel(side_ref, ids_ref, table_ref, out_ref, columns_ref):
    ids = id_columns(ids_ref, 0, side_ref[3])
    for level in range(1, LAYERS):
        columns_ref[level - 1] = id_columns(ids_ref, level, side_ref[3])
    total = jnp.zeros(out_ref.shape, jnp.float32)
    for b in range(0, table_ref.shape[0], CHUNK):
        table = table_ref[b : b + CHUNK].reshape(CHUNK * BLOCK, -1)
        total += dot(one_hot(ids, b * BLOCK, CHUNK), table)
    out_ref[...] = total.astype(out_ref.dtype)


def touch_kernel(*refs):
    refs[-1][...] = jnp.zeros_like(refs[-1])


def expand_kernel(level, place_ref, columns_ref, tiles_ref, out_ref):
    column = columns_ref[level]
    out_ref[...] = jnp.zeros_like(out_ref)

    def group(step, carry):
        for i in range(STEP):
            b = step * STEP + i
            tiles = jnp.concatenate([tiles_ref[b, k] for k in range(4)], axis=1)
            taken = dot(one_hot(column, b * BLOCK, 1), tiles).astype(jnp.bfloat16)
            for k in range(4):
                out_ref[place_ref[b * 4 + k]] += taken[:, k * BLOCK : (k + 1) * BLOCK]
        return carry

    lax.fori_loop(0, tiles_ref.shape[0] // STEP, group, 0)


def tile_sum(b, tiles_ref, blocks):
    tiles = jnp.concatenate([tiles_ref[b, k] for k in range(4)], axis=1)
    return dot(tiles, jnp.concatenate(blocks, axis=0))


def band_kernel(level, offsets_ref, side_ref, table_ref, inner_ref, outer_ref, tiles_ref, *rest):
    outs = 2 if level == 0 else 3
    extra, (out_ref, *more_refs, padded) = rest[:-outs], rest[-outs:]
    blocks = table_ref.shape[0]
    padded[BAND : BAND + blocks] = table_ref[...]
    core, has_left, has_right = side_ref[0], side_ref[1], side_ref[2]
    inner, outer = inner_ref[...], outer_ref[...]
    left = jnp.where(core == 0, outer, inner)
    right = jnp.where(core == 0, inner, outer)
    padded[0:BAND] = jnp.where(has_left == 1, left, jnp.zeros_like(left))
    padded[BAND + blocks :] = jnp.where(has_right == 1, right, jnp.zeros_like(right))
    pick_rows = 0 < level < LAYERS - 1
    more_ref = more_refs[0] if more_refs else None
    if pick_rows:
        ids = extra[0][level]
        more_ref[...] = jnp.zeros_like(more_ref)

    def group(step, carry):
        values = []
        for i in range(STEP):
            b = step * STEP + i
            near = [padded[b + BAND + offsets_ref[b * 4 + k]] for k in range(4)]
            values.append(tile_sum(b, tiles_ref, near))
            out_ref[b] = values[-1]
            if level == LAYERS - 1:
                total = table_ref[b].astype(jnp.float32)
                for ref in extra:
                    total = total + ref[b].astype(jnp.float32)
                more_ref[b] = total
        if pick_rows:
            value = jnp.concatenate(values, axis=0)
            high = value.astype(jnp.bfloat16)
            low = (value - high.astype(jnp.float32)).astype(jnp.bfloat16)
            hot = one_hot(ids, step * STEP * BLOCK, STEP)
            both = dot(hot, jnp.concatenate([high, low], axis=1))
            more_ref[...] += both[:, :BLOCK] + both[:, BLOCK:]
        return carry

    lax.fori_loop(0, blocks // STEP, group, 0)


def band_products(level, offsets, side, table, inner, outer, tiles, extra):
    blocks = table.shape[0]
    more = {0: [], LAYERS - 1: [f32(blocks, BLOCK, BLOCK)]}.get(level, [f32(BLOCK, BLOCK)])
    return call(
        functools.partial(band_kernel, level),
        [f32(blocks, BLOCK, BLOCK)] + more,
        (offsets, side),
        (table, inner, outer, tiles, *extra),
        2**29,
        [pltpu.VMEM((blocks + 2 * BAND, BLOCK, BLOCK), jnp.bfloat16)],
    )


def hub_kernel(mode, place_ref, tiles_ref, band_ref, *rest):
    panel = rest[-1]
    if mode == "pick":
        extra_ref, *pieces, out_ref, picked_ref, panel = rest
    elif mode == "mean":
        extra_ref, *pieces, out_ref, panel = rest
    else:
        *pieces, out_ref, panel = rest
    start = 0
    for ref in pieces:
        count = ref.shape[0] // BLOCK
        panel[start : start + count] = ref[...].reshape(count, BLOCK, BLOCK)
        start += count

    def group(step, total):
        values = []
        for i in range(STEP):
            b = step * STEP + i
            near = [panel[place_ref[b * 4 + k]] for k in range(4)]
            value = (tile_sum(b, tiles_ref, near) + band_ref[b]).astype(jnp.bfloat16)
            if mode == "mean":
                value = ((extra_ref[b] + value.astype(jnp.float32)) * 0.25).astype(jnp.bfloat16)
            out_ref[b] = value
            values.append(value)
        if mode == "pick":
            hot = one_hot(extra_ref[0], step * STEP * BLOCK, STEP)
            total = total + dot(hot, jnp.concatenate(values, axis=0))
        return total

    total = jnp.zeros((BLOCK, BLOCK), jnp.float32) if mode == "pick" else 0
    total = lax.fori_loop(0, tiles_ref.shape[0] // STEP, group, total)
    if mode == "pick":
        picked_ref[...] = total.astype(jnp.bfloat16)


def hub_layer(mode, place, pieces, tiles, band, *extra):
    out_shape = [bf16(tiles.shape[0], BLOCK, BLOCK)]
    if mode == "pick":
        out_shape.append(bf16(BLOCK, BLOCK))
    return call(
        functools.partial(hub_kernel, mode),
        out_shape,
        (place,),
        (tiles, band, *extra, *pieces),
        2**29,
        [pltpu.VMEM((DEVICES, BLOCK, BLOCK), jnp.bfloat16)],
    )


def row_sums(spread_ref, first, refs):
    total = None
    for ref in refs:
        count = ref.shape[0] // BLOCK
        spread = jnp.concatenate([spread_ref[first + i] for i in range(count)], axis=1)
        part = dot(spread, ref[...])
        total = part if total is None else total + part
        first += count
    return total


def part_kernel(near_ref, spread_ref, *rest):
    rest[-1][...] = near_ref[...] + row_sums(spread_ref, 0, rest[:-1])


def close_kernel(part_ref, spread_ref, piece_ref, out_ref):
    first = DEVICES - piece_ref.shape[0] // BLOCK
    out_ref[...] = (part_ref[...] + row_sums(spread_ref, first, [piece_ref])).astype(jnp.bfloat16)


def together(*arrays):
    return lax.optimization_barrier(arrays)


def body(embeddings, band_tiles, band_offsets, hub_tiles, hub_blocks, hub_ids):
    rows_dev, features = embeddings.shape
    blocks = rows_dev // BLOCK
    me = lax.axis_index("row")
    core = me % 2
    side = jnp.stack([core, (me > 0).astype(jnp.int32), (me < DEVICES - 1).astype(jnp.int32), me * rows_dev])
    offsets = band_offsets.reshape(-1)
    place = places(hub_blocks, me).reshape(-1)

    def edges(table):
        inner = lax.dynamic_slice_in_dim(table, jnp.where(core == 0, blocks - BAND, 0), BAND)
        outer = lax.dynamic_slice_in_dim(table, jnp.where(core == 0, 0, blocks - BAND), BAND)
        return inner, outer

    def exchange(rims):
        return [permute(rim, pairs) for rim, pairs in zip(rims, (ACROSS_CORE, ACROSS_EDGE))]

    table = embeddings.reshape(blocks, BLOCK, features)
    picked, columns = call(
        pick_kernel,
        [bf16(BLOCK, features), jax.ShapeDtypeStruct((LAYERS - 1, BLOCK, BLOCK), jnp.int32)],
        (side,),
        (hub_ids, table),
        2**27,
    )
    tables = [table]
    pieces = band = spread = None
    for level in range(LAYERS):
        if level == 1:
            picked, table = together(picked, table)
            across = permute(picked, along_z(6))
            halos = exchange(edges(table))
            across, *halos = together(across, *halos)
        elif level == 0:
            across = permute(picked, along_z(6))
        else:
            across = permute(picked, along_z(6))
            (table,) = hub_layer("", place, pieces, hub_tiles, band)
            across, table = together(across, table)
            tables.append(table)
        if level == 0:
            across, place, offsets = together(across, place, offsets)
        pair, columns = together(jnp.concatenate([picked, across]), columns)
        near = [permute(pair, along_z(g)) for g in (1, 2, 3)]
        if level == 0:
            held = call(touch_kernel, f32(8, BLOCK), (), (columns, hub_tiles, band_tiles), 2**20)
            near[1], held = together(near[1], held)
        elif level == 1:
            spread = call(
                functools.partial(expand_kernel, level),
                bf16(DEVICES, BLOCK, BLOCK),
                (place,),
                (columns, hub_tiles),
                2**29,
            )
            near[1], spread = together(near[1], spread)
        if level != 1:
            rims = edges(table)
            *near, rim_inner, rim_outer = together(*near, *rims)
            halos = exchange((rim_inner, rim_outer))
            (column,) = together(jnp.concatenate([pair] + near))
        else:
            column, *halos = together(jnp.concatenate([pair] + near), *halos)
        inner, outer = halos
        x_column = permute(column, ACROSS_X)
        core_column = permute(column, ACROSS_CORE)
        extra = ([held], [columns], tables[:-1])[level]
        band, *more = band_products(level, offsets, side, table, inner, outer, band_tiles, extra)
        x_column, core_column, band, *more = together(x_column, core_column, band, *more)
        far = permute(x_column, ACROSS_CORE)
        pieces = [column, x_column, core_column, far]
        if level == 0:
            table, picked = hub_layer("pick", place, pieces, hub_tiles, band, columns)
            tables.append(table)
            picked, columns, table = together(picked, columns, table)
        elif level == 1:
            part = call(part_kernel, f32(BLOCK, features), (), (more[0], spread, *pieces[:3]), 2**27)
            picked = call(close_kernel, bf16(BLOCK, features), (), (part, spread, far), 2**25)
            picked, band, *pieces = together(picked, band, *pieces)
    (averaged,) = hub_layer("mean", place, pieces, hub_tiles, band, more[0])
    return averaged.reshape(rows_dev, features)


def solution(mesh):
    return jax.shard_map(
        body,
        mesh=mesh,
        in_specs=(
            P(("group", "row"), None),
            P(("group", "row"), None, None, None),
            P(("group", "row"), None),
            P(("group", "row"), None, None, None),
            P(("group", "row"), None),
            P(None, ("group", "row")),
        ),
        out_specs=P(("group", "row"), None),
        check_vma=False,
    )
```

```python
import functools

import jax
import jax.numpy as jnp
from jax import lax
from jax.experimental import pallas as pl
from jax.experimental.pallas import tpu as pltpu
from jax.sharding import PartitionSpec as P

BAND = 3
LAYERS = 3
BLOCK = 128
STEP = 16
CHUNK = 8
DEVICES = 32


def index_of(x, z, c):
    return x * 16 + z * 2 + c


def permutation(move):
    return [
        (index_of(x, z, c), index_of(*move(x, z, c)))
        for x in range(2)
        for z in range(8)
        for c in range(2)
    ]


def along_z(step):
    return permutation(lambda x, z, c: (x, z ^ step, c))


ACROSS_X = permutation(lambda x, z, c: (1 - x, z, c))
ACROSS_CORE = permutation(lambda x, z, c: (x, z, 1 - c))
ACROSS_EDGE = [
    (i, (i + 1) % DEVICES if i % 2 else (i - 1) % DEVICES) for i in range(DEVICES)
]


def permute(array, pairs):
    return lax.ppermute(array, "row", pairs)


def places(hub_blocks, me):
    delta = hub_blocks ^ me
    dx, dz, dc = delta >> 4, (delta >> 1) & 7, delta & 1
    s = dz >> 2
    g = (dz & 3) ^ (2 * s)
    return 16 * dc + 8 * dx + 2 * g + s


def dot(a, b):
    return jnp.dot(a, b, preferred_element_type=jnp.float32)


def id_columns(ids_ref, level):
    row = ids_ref[level : level + 1, :]
    return jnp.transpose(jnp.broadcast_to(row, (BLOCK, BLOCK)))


def one_hot(ids, first, count):
    column = lax.broadcasted_iota(jnp.int32, (BLOCK, BLOCK), 1) + first
    parts = [(column + i * BLOCK == ids).astype(jnp.bfloat16) for i in range(count)]
    return jnp.concatenate(parts, axis=1)


def call(kernel, out_shape, scalars, arrays, flops, scratch=(), aliases=None):
    smem = pl.BlockSpec(memory_space=pltpu.SMEM)
    vmem = pl.BlockSpec(memory_space=pltpu.VMEM)
    moved = sum(a.size * a.dtype.itemsize for a in arrays)
    return pl.pallas_call(
        kernel,
        in_specs=[smem] * len(scalars) + [vmem] * len(arrays),
        out_specs=jax.tree.map(lambda _: vmem, out_shape),
        out_shape=out_shape,
        scratch_shapes=list(scratch),
        input_output_aliases=aliases or {},
        compiler_params=pltpu.CompilerParams(vmem_limit_bytes=8 * 2**20),
        cost_estimate=pl.CostEstimate(flops=1, bytes_accessed=1, transcendentals=0),
    )(*scalars, *arrays)


def f32(*shape):
    return jax.ShapeDtypeStruct(shape, jnp.float32)


def bf16(*shape):
    return jax.ShapeDtypeStruct(shape, jnp.bfloat16)


def pick_kernel(ids_ref, table_ref, out_ref, columns_ref):
    ids = id_columns(ids_ref, 0)
    for level in range(1, LAYERS):
        columns_ref[level - 1] = id_columns(ids_ref, level)
    total = jnp.zeros(out_ref.shape, jnp.float32)
    for b in range(0, table_ref.shape[0], CHUNK):
        table = table_ref[b : b + CHUNK].reshape(CHUNK * BLOCK, -1)
        total += dot(one_hot(ids, b * BLOCK, CHUNK), table)
    out_ref[...] = total.astype(out_ref.dtype)


def touch_kernel(*refs):
    refs[-1][...] = jnp.zeros_like(refs[-1])


def expand_kernel(level, place_ref, columns_ref, tiles_ref, out_ref):
    column = columns_ref[level]
    out_ref[...] = jnp.zeros_like(out_ref)

    def group(step, carry):
        for i in range(STEP):
            b = step * STEP + i
            tiles = jnp.concatenate([tiles_ref[b, k] for k in range(4)], axis=1)
            taken = dot(one_hot(column, b * BLOCK, 1), tiles).astype(jnp.bfloat16)
            for k in range(4):
                out_ref[place_ref[b * 4 + k]] += taken[:, k * BLOCK : (k + 1) * BLOCK]
        return carry

    lax.fori_loop(0, tiles_ref.shape[0] // STEP, group, 0)


def tile_sum(b, tiles_ref, blocks):
    tiles = jnp.concatenate([tiles_ref[b, k] for k in range(4)], axis=1)
    return dot(tiles, jnp.concatenate(blocks, axis=0))


def inner_kernel(level, offsets_ref, table_ref, tiles_ref, *rest):
    more = 1 if level == LAYERS - 1 else 0
    extra, outs = rest[: len(rest) - 1 - more], rest[len(rest) - 1 - more :]
    blocks = table_ref.shape[0]
    half = (blocks - 2 * BAND) // 2

    def group(step, carry):
        for i in range(half):
            b = BAND + step * half + i
            near = [table_ref[b + offsets_ref[b * 4 + k]] for k in range(4)]
            outs[0][b] = tile_sum(b, tiles_ref, near)
        if more:
            for i in range(blocks // 2):
                b = step * (blocks // 2) + i
                total = table_ref[b].astype(jnp.float32)
                for ref in extra:
                    total = total + ref[b].astype(jnp.float32)
                outs[1][b] = total
        return carry

    lax.fori_loop(0, 2, group, 0)


def inner_products(level, offsets, table, tiles, extra):
    blocks = table.shape[0]
    shape = f32(blocks, BLOCK, BLOCK)
    return call(
        functools.partial(inner_kernel, level),
        [shape, shape] if level == LAYERS - 1 else [shape],
        (offsets,),
        (table, tiles, *extra),
        2**29,
    )


def rim_kernel(level, offsets_ref, side_ref, band_ref, table_ref, inner_ref, outer_ref, tiles_ref, *rest):
    del band_ref
    pick_rows = level == 1
    if pick_rows:
        columns_ref, out_ref, more_ref, window = rest
    else:
        out_ref, window = rest
    blocks = table_ref.shape[0]
    core, has_left, has_right = side_ref[0], side_ref[1], side_ref[2]
    inner, outer = inner_ref[...], outer_ref[...]
    left = jnp.where(core == 0, outer, inner)
    right = jnp.where(core == 0, inner, outer)
    window[0:BAND] = jnp.where(has_left == 1, left, jnp.zeros_like(left))
    window[BAND : 3 * BAND] = table_ref[0 : 2 * BAND]
    window[3 * BAND : 5 * BAND] = table_ref[blocks - 2 * BAND :]
    window[5 * BAND :] = jnp.where(has_right == 1, right, jnp.zeros_like(right))
    for i in range(2 * BAND):
        b = i if i < BAND else blocks - 2 * BAND + i
        at = i + BAND if i < BAND else i + 3 * BAND
        near = [window[at + offsets_ref[b * 4 + k]] for k in range(4)]
        out_ref[b] = tile_sum(b, tiles_ref, near)
    if pick_rows:
        total = jnp.zeros((BLOCK, 2 * BLOCK), jnp.float32)
        for first in range(0, blocks, STEP):
            value = out_ref[first : first + STEP].reshape(STEP * BLOCK, BLOCK)
            high = value.astype(jnp.bfloat16)
            low = (value - high.astype(jnp.float32)).astype(jnp.bfloat16)
            hot = one_hot(columns_ref[level], first * BLOCK, STEP)
            total += dot(hot, jnp.concatenate([high, low], axis=1))
        more_ref[...] = total[:, :BLOCK] + total[:, BLOCK:]


def rim_products(level, offsets, side, band, table, halos, tiles, extra):
    blocks = table.shape[0]
    return call(
        functools.partial(rim_kernel, level),
        [f32(blocks, BLOCK, BLOCK)] + ([f32(BLOCK, BLOCK)] if level == 1 else []),
        (offsets, side),
        (band, table, *halos, tiles, *extra),
        2**29,
        [pltpu.VMEM((6 * BAND, BLOCK, BLOCK), jnp.bfloat16)],
        {2: 0},
    )


def hub_kernel(mode, place_ref, tiles_ref, band_ref, *rest):
    panel = rest[-1]
    if mode == "pick":
        extra_ref, *pieces, out_ref, picked_ref, panel = rest
    elif mode == "mean":
        extra_ref, *pieces, out_ref, panel = rest
    else:
        *pieces, out_ref, panel = rest
    start = 0
    for ref in pieces:
        count = ref.shape[0] // BLOCK
        panel[start : start + count] = ref[...].reshape(count, BLOCK, BLOCK)
        start += count

    def group(step, total):
        values = []
        for i in range(STEP):
            b = step * STEP + i
            near = [panel[place_ref[b * 4 + k]] for k in range(4)]
            value = (tile_sum(b, tiles_ref, near) + band_ref[b]).astype(jnp.bfloat16)
            if mode == "mean":
                value = ((extra_ref[b] + value.astype(jnp.float32)) * 0.25).astype(jnp.bfloat16)
            out_ref[b] = value
            values.append(value)
        if mode == "pick":
            hot = one_hot(extra_ref[0], step * STEP * BLOCK, STEP)
            total = total + dot(hot, jnp.concatenate(values, axis=0))
        return total

    total = jnp.zeros((BLOCK, BLOCK), jnp.float32) if mode == "pick" else 0
    total = lax.fori_loop(0, tiles_ref.shape[0] // STEP, group, total)
    if mode == "pick":
        picked_ref[...] = total.astype(jnp.bfloat16)


def hub_layer(mode, place, pieces, tiles, band, *extra):
    out_shape = [bf16(tiles.shape[0], BLOCK, BLOCK)]
    if mode == "pick":
        out_shape.append(bf16(BLOCK, BLOCK))
    return call(
        functools.partial(hub_kernel, mode),
        out_shape,
        (place,),
        (tiles, band, *extra, *pieces),
        2**29,
        [pltpu.VMEM((DEVICES, BLOCK, BLOCK), jnp.bfloat16)],
    )


def row_sums(spread_ref, first, refs):
    total = None
    for ref in refs:
        count = ref.shape[0] // BLOCK
        spread = jnp.concatenate([spread_ref[first + i] for i in range(count)], axis=1)
        part = dot(spread, ref[...])
        total = part if total is None else total + part
        first += count
    return total


def part_kernel(near_ref, spread_ref, *rest):
    rest[-1][...] = near_ref[...] + row_sums(spread_ref, 0, rest[:-1])


def close_kernel(part_ref, spread_ref, piece_ref, out_ref):
    first = DEVICES - piece_ref.shape[0] // BLOCK
    out_ref[...] = (part_ref[...] + row_sums(spread_ref, first, [piece_ref])).astype(jnp.bfloat16)


def together(*arrays):
    return lax.optimization_barrier(arrays)


def body(embeddings, band_tiles, band_offsets, hub_tiles, hub_blocks, hub_ids):
    rows_dev, features = embeddings.shape
    blocks = rows_dev // BLOCK
    me = lax.axis_index("row")
    core = me % 2
    side = jnp.stack([core, (me > 0).astype(jnp.int32), (me < DEVICES - 1).astype(jnp.int32)])
    offsets = band_offsets.reshape(-1)
    place = places(hub_blocks, me).reshape(-1)

    def edges(table):
        inner = lax.dynamic_slice_in_dim(table, jnp.where(core == 0, blocks - BAND, 0), BAND)
        outer = lax.dynamic_slice_in_dim(table, jnp.where(core == 0, 0, blocks - BAND), BAND)
        return inner, outer

    def exchange(rims):
        return [permute(rim, pairs) for rim, pairs in zip(rims, (ACROSS_CORE, ACROSS_EDGE))]

    table = embeddings.reshape(blocks, BLOCK, features)
    picked, columns = call(
        pick_kernel,
        [bf16(BLOCK, features), jax.ShapeDtypeStruct((LAYERS - 1, BLOCK, BLOCK), jnp.int32)],
        (),
        (hub_ids - me * rows_dev, table),
        2**27,
    )
    tables = [table]
    pieces = band = spread = None
    for level in range(LAYERS):
        across = permute(picked, along_z(6))
        if level == 0:
            across, place, offsets = together(across, place, offsets)
        elif level == 1:
            spread = call(
                functools.partial(expand_kernel, level),
                bf16(DEVICES, BLOCK, BLOCK),
                (place,),
                (columns, hub_tiles),
                2**29,
            )
            across, spread = together(across, spread)
        else:
            (table,) = hub_layer("", place, pieces, hub_tiles, band)
            across, table = together(across, table)
            tables.append(table)
        pair, columns = together(jnp.concatenate([picked, across]), columns)
        near = [permute(pair, along_z(g)) for g in (1, 2, 3)]
        if level == 0:
            held = call(touch_kernel, f32(8, BLOCK), (), (columns, hub_tiles, band_tiles), 2**20)
            near[1], held = together(near[1], held)
        *near, rim_inner, rim_outer, table = together(*near, *edges(table), table)
        column, table = together(jnp.concatenate([pair] + near), table)
        x_column = permute(column, ACROSS_X)
        core_column = permute(column, ACROSS_CORE)
        halos = exchange((rim_inner, rim_outer))
        extra = ([held], [], tables[:-1])[level]
        band, *base = inner_products(level, offsets, table, band_tiles, extra)
        *halos, band = together(*halos, band)
        extra = [columns] if level == 1 else []
        band, *more = rim_products(level, offsets, side, band, table, halos, band_tiles, extra)
        x_column, core_column, band, *more = together(x_column, core_column, band, *more)
        far = permute(x_column, ACROSS_CORE)
        pieces = [column, x_column, core_column, far]
        if level == 0:
            table, picked = hub_layer("pick", place, pieces, hub_tiles, band, columns)
            tables.append(table)
            picked, columns, table = together(picked, columns, table)
        elif level == 1:
            part = call(part_kernel, f32(BLOCK, features), (), (more[0], spread, *pieces[:-1]), 2**27)
            picked = call(close_kernel, bf16(BLOCK, features), (), (part, spread, far), 2**25)
            picked, band, *pieces = together(picked, band, *pieces)
    (averaged,) = hub_layer("mean", place, pieces, hub_tiles, band, base[0])
    return averaged.reshape(rows_dev, features)


def solution(mesh):
    return jax.shard_map(
        body,
        mesh=mesh,
        in_specs=(
            P(("group", "row"), None),
            P(("group", "row"), None, None, None),
            P(("group", "row"), None),
            P(("group", "row"), None, None, None),
            P(("group", "row"), None),
            P(None, ("group", "row")),
        ),
        out_specs=P(("group", "row"), None),
        check_vma=False,
    )
```

```python
import functools

import jax
import jax.numpy as jnp
from jax import lax
from jax.experimental import pallas as pl
from jax.experimental.pallas import tpu as pltpu
from jax.sharding import PartitionSpec as P

BAND = 3
LAYERS = 3
BLOCK = 128
STEP = 16
CHUNK = 8
DEVICES = 32


def index_of(x, z, c):
    return x * 16 + z * 2 + c


def permutation(move):
    return [
        (index_of(x, z, c), index_of(*move(x, z, c)))
        for x in range(2)
        for z in range(8)
        for c in range(2)
    ]


def along_z(step):
    return permutation(lambda x, z, c: (x, z ^ step, c))


ACROSS_X = permutation(lambda x, z, c: (1 - x, z, c))
ACROSS_CORE = permutation(lambda x, z, c: (x, z, 1 - c))
ACROSS_EDGE = [
    (i, (i + 1) % DEVICES if i % 2 else (i - 1) % DEVICES) for i in range(DEVICES)
]


def permute(array, pairs):
    return lax.ppermute(array, "row", pairs)


def places(hub_blocks, me):
    delta = hub_blocks ^ me
    dx, dz, dc = delta >> 4, (delta >> 1) & 7, delta & 1
    s = dz >> 2
    g = (dz & 3) ^ (2 * s)
    return 16 * dc + 8 * dx + 2 * g + s


def dot(a, b):
    return jnp.dot(a, b, preferred_element_type=jnp.float32)


def id_columns(ids_ref, level):
    row = ids_ref[level : level + 1, :]
    return jnp.transpose(jnp.broadcast_to(row, (BLOCK, BLOCK)))


def one_hot(ids, first, count):
    column = lax.broadcasted_iota(jnp.int32, (BLOCK, BLOCK), 1) + first
    parts = [(column + i * BLOCK == ids).astype(jnp.bfloat16) for i in range(count)]
    return jnp.concatenate(parts, axis=1)


def call(kernel, out_shape, scalars, arrays, flops, scratch=(), aliases=None):
    smem = pl.BlockSpec(memory_space=pltpu.SMEM)
    vmem = pl.BlockSpec(memory_space=pltpu.VMEM)
    moved = sum(a.size * a.dtype.itemsize for a in arrays)
    return pl.pallas_call(
        kernel,
        in_specs=[smem] * len(scalars) + [vmem] * len(arrays),
        out_specs=jax.tree.map(lambda _: vmem, out_shape),
        out_shape=out_shape,
        scratch_shapes=list(scratch),
        input_output_aliases=aliases or {},
        compiler_params=pltpu.CompilerParams(vmem_limit_bytes=8 * 2**20),
        cost_estimate=pl.CostEstimate(flops=1, bytes_accessed=1, transcendentals=0),
    )(*scalars, *arrays)


def f32(*shape):
    return jax.ShapeDtypeStruct(shape, jnp.float32)


def bf16(*shape):
    return jax.ShapeDtypeStruct(shape, jnp.bfloat16)


def pick_kernel(ids_ref, table_ref, out_ref, columns_ref):
    ids = id_columns(ids_ref, 0)
    for level in range(1, LAYERS):
        columns_ref[level - 1] = id_columns(ids_ref, level)
    total = jnp.zeros(out_ref.shape, jnp.float32)
    for b in range(0, table_ref.shape[0], CHUNK):
        table = table_ref[b : b + CHUNK].reshape(CHUNK * BLOCK, -1)
        total += dot(one_hot(ids, b * BLOCK, CHUNK), table)
    out_ref[...] = total.astype(out_ref.dtype)


def expand_kernel(level, place_ref, columns_ref, tiles_ref, out_ref):
    column = columns_ref[level]
    out_ref[...] = jnp.zeros_like(out_ref)

    def group(step, carry):
        for i in range(STEP):
            b = step * STEP + i
            tiles = jnp.concatenate([tiles_ref[b, k] for k in range(4)], axis=1)
            taken = dot(one_hot(column, b * BLOCK, 1), tiles).astype(jnp.bfloat16)
            for k in range(4):
                out_ref[place_ref[b * 4 + k]] += taken[:, k * BLOCK : (k + 1) * BLOCK]
        return carry

    lax.fori_loop(0, tiles_ref.shape[0] // STEP, group, 0)


def tile_sum(b, tiles_ref, blocks):
    tiles = jnp.concatenate([tiles_ref[b, k] for k in range(4)], axis=1)
    return dot(tiles, jnp.concatenate(blocks, axis=0))


def inner_kernel(level, offsets_ref, table_ref, tiles_ref, *rest):
    more = 1 if level == LAYERS - 1 else 0
    extra, outs = rest[: len(rest) - 1 - more], rest[len(rest) - 1 - more :]
    blocks = table_ref.shape[0]
    half = (blocks - 2 * BAND) // 2

    def group(step, carry):
        for i in range(half):
            b = BAND + step * half + i
            near = [table_ref[b + offsets_ref[b * 4 + k]] for k in range(4)]
            outs[0][b] = tile_sum(b, tiles_ref, near)
        if more:
            for i in range(blocks // 2):
                b = step * (blocks // 2) + i
                total = table_ref[b].astype(jnp.float32)
                for ref in extra:
                    total = total + ref[b].astype(jnp.float32)
                outs[1][b] = total
        return carry

    lax.fori_loop(0, 2, group, 0)


def inner_products(level, offsets, table, tiles, extra):
    blocks = table.shape[0]
    shape = f32(blocks, BLOCK, BLOCK)
    return call(
        functools.partial(inner_kernel, level),
        [shape, shape] if level == LAYERS - 1 else [shape],
        (offsets,),
        (table, tiles, *extra),
        2**29,
    )


def rim_kernel(level, offsets_ref, side_ref, band_ref, table_ref, inner_ref, outer_ref, tiles_ref, *rest):
    del band_ref
    pick_rows = level == 1
    if pick_rows:
        columns_ref, out_ref, more_ref, window = rest
    else:
        out_ref, window = rest
    blocks = table_ref.shape[0]
    core, has_left, has_right = side_ref[0], side_ref[1], side_ref[2]
    inner, outer = inner_ref[...], outer_ref[...]
    left = jnp.where(core == 0, outer, inner)
    right = jnp.where(core == 0, inner, outer)
    window[0:BAND] = jnp.where(has_left == 1, left, jnp.zeros_like(left))
    window[BAND : 3 * BAND] = table_ref[0 : 2 * BAND]
    window[3 * BAND : 5 * BAND] = table_ref[blocks - 2 * BAND :]
    window[5 * BAND :] = jnp.where(has_right == 1, right, jnp.zeros_like(right))
    for i in range(2 * BAND):
        b = i if i < BAND else blocks - 2 * BAND + i
        at = i + BAND if i < BAND else i + 3 * BAND
        near = [window[at + offsets_ref[b * 4 + k]] for k in range(4)]
        out_ref[b] = tile_sum(b, tiles_ref, near)
    if pick_rows:
        total = jnp.zeros((BLOCK, 2 * BLOCK), jnp.float32)
        for first in range(0, blocks, STEP):
            value = out_ref[first : first + STEP].reshape(STEP * BLOCK, BLOCK)
            high = value.astype(jnp.bfloat16)
            low = (value - high.astype(jnp.float32)).astype(jnp.bfloat16)
            hot = one_hot(columns_ref[level], first * BLOCK, STEP)
            total += dot(hot, jnp.concatenate([high, low], axis=1))
        more_ref[...] = total[:, :BLOCK] + total[:, BLOCK:]


def rim_products(level, offsets, side, band, table, halos, tiles, extra):
    blocks = table.shape[0]
    return call(
        functools.partial(rim_kernel, level),
        [f32(blocks, BLOCK, BLOCK)] + ([f32(BLOCK, BLOCK)] if level == 1 else []),
        (offsets, side),
        (band, table, *halos, tiles, *extra),
        2**29,
        [pltpu.VMEM((6 * BAND, BLOCK, BLOCK), jnp.bfloat16)],
        {2: 0},
    )


def hub_kernel(mode, place_ref, tiles_ref, band_ref, *rest):
    panel = rest[-1]
    if mode == "pick":
        extra_ref, *pieces, out_ref, picked_ref, panel = rest
    elif mode == "mean":
        extra_ref, *pieces, out_ref, panel = rest
    else:
        *pieces, out_ref, panel = rest
    start = 0
    for ref in pieces:
        count = ref.shape[0] // BLOCK
        panel[start : start + count] = ref[...].reshape(count, BLOCK, BLOCK)
        start += count

    def group(step, total):
        values = []
        for i in range(STEP):
            b = step * STEP + i
            near = [panel[place_ref[b * 4 + k]] for k in range(4)]
            value = (tile_sum(b, tiles_ref, near) + band_ref[b]).astype(jnp.bfloat16)
            if mode == "mean":
                value = ((extra_ref[b] + value.astype(jnp.float32)) * 0.25).astype(jnp.bfloat16)
            out_ref[b] = value
            values.append(value)
        if mode == "pick":
            hot = one_hot(extra_ref[0], step * STEP * BLOCK, STEP)
            total = total + dot(hot, jnp.concatenate(values, axis=0))
        return total

    total = jnp.zeros((BLOCK, BLOCK), jnp.float32) if mode == "pick" else 0
    total = lax.fori_loop(0, tiles_ref.shape[0] // STEP, group, total)
    if mode == "pick":
        picked_ref[...] = total.astype(jnp.bfloat16)


def hub_layer(mode, place, pieces, tiles, band, *extra):
    out_shape = [bf16(tiles.shape[0], BLOCK, BLOCK)]
    if mode == "pick":
        out_shape.append(bf16(BLOCK, BLOCK))
    return call(
        functools.partial(hub_kernel, mode),
        out_shape,
        (place,),
        (tiles, band, *extra, *pieces),
        2**29,
        [pltpu.VMEM((DEVICES, BLOCK, BLOCK), jnp.bfloat16)],
    )


def row_sums(spread_ref, first, refs):
    total = None
    for ref in refs:
        count = ref.shape[0] // BLOCK
        spread = jnp.concatenate([spread_ref[first + i] for i in range(count)], axis=1)
        part = dot(spread, ref[...])
        total = part if total is None else total + part
        first += count
    return total


def part_kernel(near_ref, spread_ref, *rest):
    rest[-1][...] = near_ref[...] + row_sums(spread_ref, 0, rest[:-1])


def close_kernel(part_ref, spread_ref, piece_ref, out_ref):
    first = DEVICES - piece_ref.shape[0] // BLOCK
    out_ref[...] = (part_ref[...] + row_sums(spread_ref, first, [piece_ref])).astype(jnp.bfloat16)


def together(*arrays):
    return lax.optimization_barrier(arrays)


def body(embeddings, band_tiles, band_offsets, hub_tiles, hub_blocks, hub_ids):
    rows_dev, features = embeddings.shape
    blocks = rows_dev // BLOCK
    me = lax.axis_index("row")
    core = me % 2
    side = jnp.stack([core, (me > 0).astype(jnp.int32), (me < DEVICES - 1).astype(jnp.int32)])
    offsets = band_offsets.reshape(-1)
    place = places(hub_blocks, me).reshape(-1)

    def edges(table):
        inner = lax.dynamic_slice_in_dim(table, jnp.where(core == 0, blocks - BAND, 0), BAND)
        outer = lax.dynamic_slice_in_dim(table, jnp.where(core == 0, 0, blocks - BAND), BAND)
        return inner, outer

    def exchange(rims):
        return [permute(rim, pairs) for rim, pairs in zip(rims, (ACROSS_CORE, ACROSS_EDGE))]

    table = embeddings.reshape(blocks, BLOCK, features)
    picked, columns = call(
        pick_kernel,
        [bf16(BLOCK, features), jax.ShapeDtypeStruct((LAYERS - 1, BLOCK, BLOCK), jnp.int32)],
        (),
        (hub_ids - me * rows_dev, table),
        2**27,
    )
    tables = [table]
    pieces = band = spread = None
    for level in range(LAYERS):
        across = permute(picked, along_z(6))
        if level == 0:
            across, place, offsets = together(across, place, offsets)
        elif level == 1:
            spread = call(
                functools.partial(expand_kernel, level),
                bf16(DEVICES, BLOCK, BLOCK),
                (place,),
                (columns, hub_tiles),
                2**29,
            )
            across, spread = together(across, spread)
        else:
            (table,) = hub_layer("", place, pieces, hub_tiles, band)
            across, table = together(across, table)
            tables.append(table)
        pair, columns = together(jnp.concatenate([picked, across]), columns)
        near = [permute(pair, along_z(g)) for g in (1, 2, 3)]
        *near, rim_inner, rim_outer, table = together(*near, *edges(table), table)
        column, table = together(jnp.concatenate([pair] + near), table)
        x_column = permute(column, ACROSS_X)
        halos = exchange((rim_inner, rim_outer))
        extra = ([], [], tables[:-1])[level]
        band, *base = inner_products(level, offsets, table, band_tiles, extra)
        *halos, band = together(*halos, band)
        extra = [columns] if level == 1 else []
        band, *more = rim_products(level, offsets, side, band, table, halos, band_tiles, extra)
        core_in, band, *more = together(column, band, *more)
        core_column = permute(core_in, ACROSS_CORE)
        far = permute(x_column, ACROSS_CORE)
        pieces = [column, x_column, core_column, far]
        if level == 0:
            table, picked = hub_layer("pick", place, pieces, hub_tiles, band, columns)
            tables.append(table)
            picked, columns, table = together(picked, columns, table)
        elif level == 1:
            part = call(part_kernel, f32(BLOCK, features), (), (more[0], spread, *pieces[:-1]), 2**27)
            picked = call(close_kernel, bf16(BLOCK, features), (), (part, spread, far), 2**25)
            picked, band, *pieces = together(picked, band, *pieces)
    (averaged,) = hub_layer("mean", place, pieces, hub_tiles, band, base[0])
    return averaged.reshape(rows_dev, features)


def solution(mesh):
    return jax.shard_map(
        body,
        mesh=mesh,
        in_specs=(
            P(("group", "row"), None),
            P(("group", "row"), None, None, None),
            P(("group", "row"), None),
            P(("group", "row"), None, None, None),
            P(("group", "row"), None),
            P(None, ("group", "row")),
        ),
        out_specs=P(("group", "row"), None),
        check_vma=False,
    )
```

```python
import functools

import jax
import jax.numpy as jnp
from jax import lax
from jax.experimental import pallas as pl
from jax.experimental.pallas import tpu as pltpu
from jax.sharding import PartitionSpec as P

BAND = 3
LAYERS = 3
BLOCK = 128
STEP = 16
CHUNK = 8
DEVICES = 32


def index_of(x, z, c):
    return x * 16 + z * 2 + c


def permutation(move):
    return [
        (index_of(x, z, c), index_of(*move(x, z, c)))
        for x in range(2)
        for z in range(8)
        for c in range(2)
    ]


def along_z(step):
    return permutation(lambda x, z, c: (x, z ^ step, c))


ACROSS_X = permutation(lambda x, z, c: (1 - x, z, c))
ACROSS_CORE = permutation(lambda x, z, c: (x, z, 1 - c))
ACROSS_EDGE = [
    (i, (i + 1) % DEVICES if i % 2 else (i - 1) % DEVICES) for i in range(DEVICES)
]


def permute(array, pairs):
    return lax.ppermute(array, "row", pairs)


def places(hub_blocks, me):
    delta = hub_blocks ^ me
    dx, dz, dc = delta >> 4, (delta >> 1) & 7, delta & 1
    s = dz >> 2
    g = (dz & 3) ^ (2 * s)
    return 16 * dc + 8 * dx + 2 * g + s


def dot(a, b):
    return jnp.dot(a, b, preferred_element_type=jnp.float32)


def id_columns(ids_ref, level):
    row = ids_ref[level : level + 1, :]
    return jnp.transpose(jnp.broadcast_to(row, (BLOCK, BLOCK)))


def one_hot(ids, first, count):
    column = lax.broadcasted_iota(jnp.int32, (BLOCK, BLOCK), 1) + first
    parts = [(column + i * BLOCK == ids).astype(jnp.bfloat16) for i in range(count)]
    return jnp.concatenate(parts, axis=1)


def call(kernel, out_shape, scalars, arrays, flops, scratch=(), aliases=None):
    smem = pl.BlockSpec(memory_space=pltpu.SMEM)
    vmem = pl.BlockSpec(memory_space=pltpu.VMEM)
    moved = sum(a.size * a.dtype.itemsize for a in arrays)
    return pl.pallas_call(
        kernel,
        in_specs=[smem] * len(scalars) + [vmem] * len(arrays),
        out_specs=jax.tree.map(lambda _: vmem, out_shape),
        out_shape=out_shape,
        scratch_shapes=list(scratch),
        input_output_aliases=aliases or {},
        compiler_params=pltpu.CompilerParams(vmem_limit_bytes=8 * 2**20),
        cost_estimate=pl.CostEstimate(flops=1, bytes_accessed=1, transcendentals=0),
    )(*scalars, *arrays)


def f32(*shape):
    return jax.ShapeDtypeStruct(shape, jnp.float32)


def bf16(*shape):
    return jax.ShapeDtypeStruct(shape, jnp.bfloat16)


def pick_kernel(ids_ref, table_ref, out_ref, columns_ref):
    ids = id_columns(ids_ref, 0)
    for level in range(1, LAYERS):
        columns_ref[level - 1] = id_columns(ids_ref, level)
    total = jnp.zeros(out_ref.shape, jnp.float32)
    for b in range(0, table_ref.shape[0], CHUNK):
        table = table_ref[b : b + CHUNK].reshape(CHUNK * BLOCK, -1)
        total += dot(one_hot(ids, b * BLOCK, CHUNK), table)
    out_ref[...] = total.astype(out_ref.dtype)


def expand_kernel(level, place_ref, columns_ref, tiles_ref, out_ref):
    column = columns_ref[level]
    out_ref[...] = jnp.zeros_like(out_ref)

    def group(step, carry):
        for i in range(STEP):
            b = step * STEP + i
            tiles = jnp.concatenate([tiles_ref[b, k] for k in range(4)], axis=1)
            taken = dot(one_hot(column, b * BLOCK, 1), tiles).astype(jnp.bfloat16)
            for k in range(4):
                out_ref[place_ref[b * 4 + k]] += taken[:, k * BLOCK : (k + 1) * BLOCK]
        return carry

    lax.fori_loop(0, tiles_ref.shape[0] // STEP, group, 0)


def tile_sum(b, tiles_ref, blocks):
    tiles = jnp.concatenate([tiles_ref[b, k] for k in range(4)], axis=1)
    return dot(tiles, jnp.concatenate(blocks, axis=0))


def inner_kernel(level, offsets_ref, table_ref, tiles_ref, *rest):
    more = 1 if level == LAYERS - 1 else 0
    extra, outs = rest[: len(rest) - 1 - more], rest[len(rest) - 1 - more :]
    blocks = table_ref.shape[0]
    half = (blocks - 2 * BAND) // 2

    def group(step, carry):
        for i in range(half):
            b = BAND + step * half + i
            near = [table_ref[b + offsets_ref[b * 4 + k]] for k in range(4)]
            outs[0][b] = tile_sum(b, tiles_ref, near)
        if more:
            for i in range(blocks // 2):
                b = step * (blocks // 2) + i
                total = table_ref[b].astype(jnp.float32)
                for ref in extra:
                    total = total + ref[b].astype(jnp.float32)
                outs[1][b] = total
        return carry

    lax.fori_loop(0, 2, group, 0)


def inner_products(level, offsets, table, tiles, extra):
    blocks = table.shape[0]
    shape = f32(blocks, BLOCK, BLOCK)
    return call(
        functools.partial(inner_kernel, level),
        [shape, shape] if level == LAYERS - 1 else [shape],
        (offsets,),
        (table, tiles, *extra),
        2**29,
    )


def rim_kernel(level, offsets_ref, side_ref, band_ref, table_ref, inner_ref, outer_ref, tiles_ref, *rest):
    del band_ref
    pick_rows = level == 1
    if pick_rows:
        columns_ref, out_ref, more_ref, window = rest
    else:
        out_ref, window = rest
    blocks = table_ref.shape[0]
    core, has_left, has_right = side_ref[0], side_ref[1], side_ref[2]
    inner, outer = inner_ref[...], outer_ref[...]
    left = jnp.where(core == 0, outer, inner)
    right = jnp.where(core == 0, inner, outer)
    window[0:BAND] = jnp.where(has_left == 1, left, jnp.zeros_like(left))
    window[BAND : 3 * BAND] = table_ref[0 : 2 * BAND]
    window[3 * BAND : 5 * BAND] = table_ref[blocks - 2 * BAND :]
    window[5 * BAND :] = jnp.where(has_right == 1, right, jnp.zeros_like(right))
    for i in range(2 * BAND):
        b = i if i < BAND else blocks - 2 * BAND + i
        at = i + BAND if i < BAND else i + 3 * BAND
        near = [window[at + offsets_ref[b * 4 + k]] for k in range(4)]
        out_ref[b] = tile_sum(b, tiles_ref, near)
    if pick_rows:
        total = jnp.zeros((BLOCK, 2 * BLOCK), jnp.float32)
        for first in range(0, blocks, STEP):
            value = out_ref[first : first + STEP].reshape(STEP * BLOCK, BLOCK)
            high = value.astype(jnp.bfloat16)
            low = (value - high.astype(jnp.float32)).astype(jnp.bfloat16)
            hot = one_hot(columns_ref[level], first * BLOCK, STEP)
            total += dot(hot, jnp.concatenate([high, low], axis=1))
        more_ref[...] = total[:, :BLOCK] + total[:, BLOCK:]


def rim_products(level, offsets, side, band, table, halos, tiles, extra):
    blocks = table.shape[0]
    return call(
        functools.partial(rim_kernel, level),
        [f32(blocks, BLOCK, BLOCK)] + ([f32(BLOCK, BLOCK)] if level == 1 else []),
        (offsets, side),
        (band, table, *halos, tiles, *extra),
        2**29,
        [pltpu.VMEM((6 * BAND, BLOCK, BLOCK), jnp.bfloat16)],
        {2: 0},
    )


def hub_kernel(mode, place_ref, tiles_ref, band_ref, *rest):
    panel = rest[-1]
    if mode == "pick":
        extra_ref, *pieces, out_ref, picked_ref, panel = rest
    elif mode == "mean":
        extra_ref, *pieces, out_ref, panel = rest
    else:
        *pieces, out_ref, panel = rest
    start = 0
    for ref in pieces:
        count = ref.shape[0] // BLOCK
        panel[start : start + count] = ref[...].reshape(count, BLOCK, BLOCK)
        start += count

    def group(step, total):
        values = []
        for i in range(STEP):
            b = step * STEP + i
            near = [panel[place_ref[b * 4 + k]] for k in range(4)]
            value = (tile_sum(b, tiles_ref, near) + band_ref[b]).astype(jnp.bfloat16)
            if mode == "mean":
                value = ((extra_ref[b] + value.astype(jnp.float32)) * 0.25).astype(jnp.bfloat16)
            out_ref[b] = value
            values.append(value)
        if mode == "pick":
            hot = one_hot(extra_ref[0], step * STEP * BLOCK, STEP)
            total = total + dot(hot, jnp.concatenate(values, axis=0))
        return total

    total = jnp.zeros((BLOCK, BLOCK), jnp.float32) if mode == "pick" else 0
    total = lax.fori_loop(0, tiles_ref.shape[0] // STEP, group, total)
    if mode == "pick":
        picked_ref[...] = total.astype(jnp.bfloat16)


def hub_layer(mode, place, pieces, tiles, band, *extra):
    out_shape = [bf16(tiles.shape[0], BLOCK, BLOCK)]
    if mode == "pick":
        out_shape.append(bf16(BLOCK, BLOCK))
    return call(
        functools.partial(hub_kernel, mode),
        out_shape,
        (place,),
        (tiles, band, *extra, *pieces),
        2**29,
        [pltpu.VMEM((DEVICES, BLOCK, BLOCK), jnp.bfloat16)],
    )


def row_sums(spread_ref, first, refs):
    total = None
    for ref in refs:
        count = ref.shape[0] // BLOCK
        spread = jnp.concatenate([spread_ref[first + i] for i in range(count)], axis=1)
        part = dot(spread, ref[...])
        total = part if total is None else total + part
        first += count
    return total


def part_kernel(near_ref, spread_ref, *rest):
    rest[-1][...] = near_ref[...] + row_sums(spread_ref, 0, rest[:-1])


def close_kernel(part_ref, spread_ref, piece_ref, out_ref):
    first = DEVICES - piece_ref.shape[0] // BLOCK
    out_ref[...] = (part_ref[...] + row_sums(spread_ref, first, [piece_ref])).astype(jnp.bfloat16)


def together(*arrays):
    return lax.optimization_barrier(arrays)


def body(embeddings, band_tiles, band_offsets, hub_tiles, hub_blocks, hub_ids):
    rows_dev, features = embeddings.shape
    blocks = rows_dev // BLOCK
    me = lax.axis_index("row")
    core = me % 2
    side = jnp.stack([core, (me > 0).astype(jnp.int32), (me < DEVICES - 1).astype(jnp.int32)])
    offsets = band_offsets.reshape(-1)
    place = places(hub_blocks, me).reshape(-1)

    def edges(table):
        inner = lax.dynamic_slice_in_dim(table, jnp.where(core == 0, blocks - BAND, 0), BAND)
        outer = lax.dynamic_slice_in_dim(table, jnp.where(core == 0, 0, blocks - BAND), BAND)
        return inner, outer

    def exchange(rims):
        outer = permute(rims[1], ACROSS_EDGE)
        return [permute(rims[0], ACROSS_CORE), outer]

    table = embeddings.reshape(blocks, BLOCK, features)
    picked, columns = call(
        pick_kernel,
        [bf16(BLOCK, features), jax.ShapeDtypeStruct((LAYERS - 1, BLOCK, BLOCK), jnp.int32)],
        (),
        (hub_ids - me * rows_dev, table),
        2**27,
    )
    tables = [table]
    pieces = band = spread = None
    for level in range(LAYERS):
        across = permute(picked, along_z(6))
        if level == 0:
            across, place, offsets = together(across, place, offsets)
        elif level == 1:
            spread = call(
                functools.partial(expand_kernel, level),
                bf16(DEVICES, BLOCK, BLOCK),
                (place,),
                (columns, hub_tiles),
                2**29,
            )
            across, spread = together(across, spread)
        else:
            (table,) = hub_layer("", place, pieces, hub_tiles, band)
            across, table = together(across, table)
            tables.append(table)
        pair, columns = together(jnp.concatenate([picked, across]), columns)
        near = [permute(pair, along_z(g)) for g in (1, 2, 3)]
        *near, rim_inner, rim_outer, table = together(*near, *edges(table), table)
        column, table = together(jnp.concatenate([pair] + near), table)
        x_column = permute(column, ACROSS_X)
        halos = exchange((rim_inner, rim_outer))
        extra = ([], [], tables[:-1])[level]
        band, *base = inner_products(level, offsets, table, band_tiles, extra)
        outer, inner, band = together(halos[1], halos[0], band)
        halos = [inner, outer]
        extra = [columns] if level == 1 else []
        band, *more = rim_products(level, offsets, side, band, table, halos, band_tiles, extra)
        core_in, band, *more = together(column, band, *more)
        core_column = permute(core_in, ACROSS_CORE)
        far = permute(x_column, ACROSS_CORE)
        pieces = [column, x_column, core_column, far]
        if level == 0:
            table, picked = hub_layer("pick", place, pieces, hub_tiles, band, columns)
            tables.append(table)
            picked, columns, table = together(picked, columns, table)
        elif level == 1:
            part = call(part_kernel, f32(BLOCK, features), (), (more[0], spread, *pieces[:-1]), 2**27)
            picked = call(close_kernel, bf16(BLOCK, features), (), (part, spread, far), 2**25)
            picked, band, *pieces = together(picked, band, *pieces)
    (averaged,) = hub_layer("mean", place, pieces, hub_tiles, band, base[0])
    return averaged.reshape(rows_dev, features)


def solution(mesh):
    return jax.shard_map(
        body,
        mesh=mesh,
        in_specs=(
            P(("group", "row"), None),
            P(("group", "row"), None, None, None),
            P(("group", "row"), None),
            P(("group", "row"), None, None, None),
            P(("group", "row"), None),
            P(None, ("group", "row")),
        ),
        out_specs=P(("group", "row"), None),
        check_vma=False,
    )
```

```python
import functools

import jax
import jax.numpy as jnp
from jax import lax
from jax.experimental import pallas as pl
from jax.experimental.pallas import tpu as pltpu
from jax.sharding import PartitionSpec as P

BAND = 3
LAYERS = 3
BLOCK = 128
STEP = 32
CHUNK = 8
DEVICES = 32


def index_of(x, z, c):
    return x * 16 + z * 2 + c


def permutation(move):
    return [
        (index_of(x, z, c), index_of(*move(x, z, c)))
        for x in range(2)
        for z in range(8)
        for c in range(2)
    ]


def along_z(step):
    return permutation(lambda x, z, c: (x, z ^ step, c))


ACROSS_X = permutation(lambda x, z, c: (1 - x, z, c))
ACROSS_CORE = permutation(lambda x, z, c: (x, z, 1 - c))
ACROSS_EDGE = [
    (i, (i + 1) % DEVICES if i % 2 else (i - 1) % DEVICES) for i in range(DEVICES)
]


def permute(array, pairs):
    return lax.ppermute(array, "row", pairs)


def places(hub_blocks, me):
    delta = hub_blocks ^ me
    dx, dz, dc = delta >> 4, (delta >> 1) & 7, delta & 1
    s = dz >> 2
    g = (dz & 3) ^ (2 * s)
    return 16 * dc + 8 * dx + 2 * g + s


def dot(a, b):
    return jnp.dot(a, b, preferred_element_type=jnp.float32)


def id_columns(ids_ref, level):
    row = ids_ref[level : level + 1, :]
    return jnp.transpose(jnp.broadcast_to(row, (BLOCK, BLOCK)))


def one_hot(ids, first, count):
    column = lax.broadcasted_iota(jnp.int32, (BLOCK, BLOCK), 1) + first
    parts = [(column + i * BLOCK == ids).astype(jnp.bfloat16) for i in range(count)]
    return jnp.concatenate(parts, axis=1)


def call(kernel, out_shape, scalars, arrays, flops, scratch=(), aliases=None):
    smem = pl.BlockSpec(memory_space=pltpu.SMEM)
    vmem = pl.BlockSpec(memory_space=pltpu.VMEM)
    moved = sum(a.size * a.dtype.itemsize for a in arrays)
    return pl.pallas_call(
        kernel,
        in_specs=[smem] * len(scalars) + [vmem] * len(arrays),
        out_specs=jax.tree.map(lambda _: vmem, out_shape),
        out_shape=out_shape,
        scratch_shapes=list(scratch),
        input_output_aliases=aliases or {},
        compiler_params=pltpu.CompilerParams(vmem_limit_bytes=8 * 2**20),
        cost_estimate=pl.CostEstimate(flops=1, bytes_accessed=1, transcendentals=0),
    )(*scalars, *arrays)


def f32(*shape):
    return jax.ShapeDtypeStruct(shape, jnp.float32)


def bf16(*shape):
    return jax.ShapeDtypeStruct(shape, jnp.bfloat16)


def pick_kernel(ids_ref, table_ref, out_ref, columns_ref):
    ids = id_columns(ids_ref, 0)
    for level in range(1, LAYERS):
        columns_ref[level - 1] = id_columns(ids_ref, level)
    total = jnp.zeros(out_ref.shape, jnp.float32)
    for b in range(0, table_ref.shape[0], CHUNK):
        table = table_ref[b : b + CHUNK].reshape(CHUNK * BLOCK, -1)
        total += dot(one_hot(ids, b * BLOCK, CHUNK), table)
    out_ref[...] = total.astype(out_ref.dtype)


def expand_kernel(level, place_ref, columns_ref, tiles_ref, out_ref):
    column = columns_ref[level]
    out_ref[...] = jnp.zeros_like(out_ref)

    def group(step, carry):
        for i in range(STEP):
            b = step * STEP + i
            tiles = jnp.concatenate([tiles_ref[b, k] for k in range(4)], axis=1)
            taken = dot(one_hot(column, b * BLOCK, 1), tiles).astype(jnp.bfloat16)
            for k in range(4):
                out_ref[place_ref[b * 4 + k]] += taken[:, k * BLOCK : (k + 1) * BLOCK]
        return carry

    lax.fori_loop(0, tiles_ref.shape[0] // STEP, group, 0)


def tile_sum(b, tiles_ref, blocks):
    tiles = jnp.concatenate([tiles_ref[b, k] for k in range(4)], axis=1)
    return dot(tiles, jnp.concatenate(blocks, axis=0))


def inner_kernel(level, offsets_ref, table_ref, tiles_ref, *rest):
    more = 1 if level == LAYERS - 1 else 0
    extra, outs = rest[: len(rest) - 1 - more], rest[len(rest) - 1 - more :]
    blocks = table_ref.shape[0]
    half = (blocks - 2 * BAND) // 2

    def group(step, carry):
        for i in range(half):
            b = BAND + step * half + i
            near = [table_ref[b + offsets_ref[b * 4 + k]] for k in range(4)]
            outs[0][b] = tile_sum(b, tiles_ref, near)
        if more:
            for i in range(blocks // 2):
                b = step * (blocks // 2) + i
                total = table_ref[b].astype(jnp.float32)
                for ref in extra:
                    total = total + ref[b].astype(jnp.float32)
                outs[1][b] = total
        return carry

    lax.fori_loop(0, 2, group, 0)


def inner_products(level, offsets, table, tiles, extra):
    blocks = table.shape[0]
    shape = f32(blocks, BLOCK, BLOCK)
    return call(
        functools.partial(inner_kernel, level),
        [shape, shape] if level == LAYERS - 1 else [shape],
        (offsets,),
        (table, tiles, *extra),
        2**29,
    )


def rim_kernel(level, offsets_ref, side_ref, band_ref, table_ref, inner_ref, outer_ref, tiles_ref, *rest):
    del band_ref
    pick_rows = level == 1
    if pick_rows:
        columns_ref, out_ref, more_ref, window = rest
    else:
        out_ref, window = rest
    blocks = table_ref.shape[0]
    core, has_left, has_right = side_ref[0], side_ref[1], side_ref[2]
    inner, outer = inner_ref[...], outer_ref[...]
    left = jnp.where(core == 0, outer, inner)
    right = jnp.where(core == 0, inner, outer)
    window[0:BAND] = jnp.where(has_left == 1, left, jnp.zeros_like(left))
    window[BAND : 3 * BAND] = table_ref[0 : 2 * BAND]
    window[3 * BAND : 5 * BAND] = table_ref[blocks - 2 * BAND :]
    window[5 * BAND :] = jnp.where(has_right == 1, right, jnp.zeros_like(right))
    for i in range(2 * BAND):
        b = i if i < BAND else blocks - 2 * BAND + i
        at = i + BAND if i < BAND else i + 3 * BAND
        near = [window[at + offsets_ref[b * 4 + k]] for k in range(4)]
        out_ref[b] = tile_sum(b, tiles_ref, near)
    if pick_rows:
        total = jnp.zeros((BLOCK, 2 * BLOCK), jnp.float32)
        for first in range(0, blocks, STEP):
            value = out_ref[first : first + STEP].reshape(STEP * BLOCK, BLOCK)
            high = value.astype(jnp.bfloat16)
            low = (value - high.astype(jnp.float32)).astype(jnp.bfloat16)
            hot = one_hot(columns_ref[level], first * BLOCK, STEP)
            total += dot(hot, jnp.concatenate([high, low], axis=1))
        more_ref[...] = total[:, :BLOCK] + total[:, BLOCK:]


def rim_products(level, offsets, side, band, table, halos, tiles, extra):
    blocks = table.shape[0]
    return call(
        functools.partial(rim_kernel, level),
        [f32(blocks, BLOCK, BLOCK)] + ([f32(BLOCK, BLOCK)] if level == 1 else []),
        (offsets, side),
        (band, table, *halos, tiles, *extra),
        2**29,
        [pltpu.VMEM((6 * BAND, BLOCK, BLOCK), jnp.bfloat16)],
        {2: 0},
    )


def hub_kernel(mode, place_ref, tiles_ref, band_ref, *rest):
    panel = rest[-1]
    if mode == "pick":
        extra_ref, *pieces, out_ref, picked_ref, panel = rest
    elif mode == "mean":
        extra_ref, *pieces, out_ref, panel = rest
    else:
        *pieces, out_ref, panel = rest
    start = 0
    for ref in pieces:
        count = ref.shape[0] // BLOCK
        panel[start : start + count] = ref[...].reshape(count, BLOCK, BLOCK)
        start += count

    def group(step, total):
        values = []
        for i in range(STEP):
            b = step * STEP + i
            near = [panel[place_ref[b * 4 + k]] for k in range(4)]
            value = (tile_sum(b, tiles_ref, near) + band_ref[b]).astype(jnp.bfloat16)
            if mode == "mean":
                value = ((extra_ref[b] + value.astype(jnp.float32)) * 0.25).astype(jnp.bfloat16)
            out_ref[b] = value
            values.append(value)
        if mode == "pick":
            hot = one_hot(extra_ref[0], step * STEP * BLOCK, STEP)
            total = total + dot(hot, jnp.concatenate(values, axis=0))
        return total

    total = jnp.zeros((BLOCK, BLOCK), jnp.float32) if mode == "pick" else 0
    total = lax.fori_loop(0, tiles_ref.shape[0] // STEP, group, total)
    if mode == "pick":
        picked_ref[...] = total.astype(jnp.bfloat16)


def hub_layer(mode, place, pieces, tiles, band, *extra):
    out_shape = [bf16(tiles.shape[0], BLOCK, BLOCK)]
    if mode == "pick":
        out_shape.append(bf16(BLOCK, BLOCK))
    return call(
        functools.partial(hub_kernel, mode),
        out_shape,
        (place,),
        (tiles, band, *extra, *pieces),
        2**29,
        [pltpu.VMEM((DEVICES, BLOCK, BLOCK), jnp.bfloat16)],
    )


def row_sums(spread_ref, first, refs):
    total = None
    for ref in refs:
        count = ref.shape[0] // BLOCK
        spread = jnp.concatenate([spread_ref[first + i] for i in range(count)], axis=1)
        part = dot(spread, ref[...])
        total = part if total is None else total + part
        first += count
    return total


def part_kernel(near_ref, spread_ref, *rest):
    rest[-1][...] = near_ref[...] + row_sums(spread_ref, 0, rest[:-1])


def close_kernel(part_ref, spread_ref, piece_ref, out_ref):
    first = DEVICES - piece_ref.shape[0] // BLOCK
    out_ref[...] = (part_ref[...] + row_sums(spread_ref, first, [piece_ref])).astype(jnp.bfloat16)


def together(*arrays):
    return lax.optimization_barrier(arrays)


def body(embeddings, band_tiles, band_offsets, hub_tiles, hub_blocks, hub_ids):
    rows_dev, features = embeddings.shape
    blocks = rows_dev // BLOCK
    me = lax.axis_index("row")
    core = me % 2
    side = jnp.stack([core, (me > 0).astype(jnp.int32), (me < DEVICES - 1).astype(jnp.int32)])
    offsets = band_offsets.reshape(-1)
    place = places(hub_blocks, me).reshape(-1)

    def edges(table):
        inner = lax.dynamic_slice_in_dim(table, jnp.where(core == 0, blocks - BAND, 0), BAND)
        outer = lax.dynamic_slice_in_dim(table, jnp.where(core == 0, 0, blocks - BAND), BAND)
        return inner, outer

    def exchange(rims):
        outer = permute(rims[1], ACROSS_EDGE)
        return [permute(rims[0], ACROSS_CORE), outer]

    table = embeddings.reshape(blocks, BLOCK, features)
    picked, columns = call(
        pick_kernel,
        [bf16(BLOCK, features), jax.ShapeDtypeStruct((LAYERS - 1, BLOCK, BLOCK), jnp.int32)],
        (),
        (hub_ids - me * rows_dev, table),
        2**27,
    )
    tables = [table]
    pieces = band = spread = None
    for level in range(LAYERS):
        across = permute(picked, along_z(6))
        if level == 0:
            across, place, offsets = together(across, place, offsets)
        elif level == 1:
            spread = call(
                functools.partial(expand_kernel, level),
                bf16(DEVICES, BLOCK, BLOCK),
                (place,),
                (columns, hub_tiles),
                2**29,
            )
            across, spread = together(across, spread)
        else:
            (table,) = hub_layer("", place, pieces, hub_tiles, band)
            across, table = together(across, table)
            tables.append(table)
        pair, columns = together(jnp.concatenate([picked, across]), columns)
        near = [permute(pair, along_z(g)) for g in (1, 2, 3)]
        *near, rim_inner, rim_outer, table = together(*near, *edges(table), table)
        column, table = together(jnp.concatenate([pair] + near), table)
        x_column = permute(column, ACROSS_X)
        halos = exchange((rim_inner, rim_outer))
        extra = ([], [], tables[:-1])[level]
        band, *base = inner_products(level, offsets, table, band_tiles, extra)
        outer, inner, band = together(halos[1], halos[0], band)
        halos = [inner, outer]
        extra = [columns] if level == 1 else []
        band, *more = rim_products(level, offsets, side, band, table, halos, band_tiles, extra)
        core_in, band, *more = together(column, band, *more)
        core_column = permute(core_in, ACROSS_CORE)
        far = permute(x_column, ACROSS_CORE)
        pieces = [column, x_column, core_column, far]
        if level == 0:
            table, picked = hub_layer("pick", place, pieces, hub_tiles, band, columns)
            tables.append(table)
            picked, columns, table = together(picked, columns, table)
        elif level == 1:
            part = call(part_kernel, f32(BLOCK, features), (), (more[0], spread, *pieces[:-1]), 2**27)
            picked = call(close_kernel, bf16(BLOCK, features), (), (part, spread, far), 2**25)
            picked, band, *pieces = together(picked, band, *pieces)
    (averaged,) = hub_layer("mean", place, pieces, hub_tiles, band, base[0])
    return averaged.reshape(rows_dev, features)


def solution(mesh):
    return jax.shard_map(
        body,
        mesh=mesh,
        in_specs=(
            P(("group", "row"), None),
            P(("group", "row"), None, None, None),
            P(("group", "row"), None),
            P(("group", "row"), None, None, None),
            P(("group", "row"), None),
            P(None, ("group", "row")),
        ),
        out_specs=P(("group", "row"), None),
        check_vma=False,
    )
```
